32 devices in a mesh: slab: 4 (over x, core), cout: 2 (over y), cin: 4 (over z).
Axes of the slice: x: 2, y: 2, z: 4, core: 2. Of those that a mesh axis runs over, the one named last changes fastest.
Arguments:
- image_in: float32 [32, 64, 2048], P('slab', None, 'cin'), may hold values from -6 to 6
- first_weight: float32 [3, 3, 2048, 2048], P(None, None, 'cin', 'cout'), may hold values from -0.046875 to 0.046875
- second_weight: float32 [3, 3, 2048, 2048], P(None, None, 'cout', 'cin'), may hold values from -0.046875 to 0.046875
- out_grad: float32 [32, 64, 2048], P('slab', None, 'cin'), may hold values from -0.13258252 to 0.13258252
Outputs:
- output: float32 [32, 64, 2048], P('slab', 'cout', 'cin')
- weight_grad: float32 [3, 3, 2048, 2048], P(None, None, ('cout', 'slab'), 'cin')
The draws below stay inside these ranges and needn't reach their ends.
All inputs are finite; a program needn't handle non-finite values.
Results may differ from the reference program's by a relative error of at most 0.0001.
Values sent between devices are 32-bit elements; how exact they have to be, the bound alone decides.
A program may use at most 128 MiB of HBM per device.

```python
import jax
import jax.numpy as jnp
from jax import lax

C = 2048
WIDTH = 64
ROWS_DEV = 8
HEIGHT = 32
N_SLAB = 4


def shard_levels(rng, dims, pieces, low, top_value):
    gain = 1.0
    for axis_at, parts in pieces:
        draws = jax.random.uniform(jax.random.fold_in(jax.random.fold_in(rng, 6), axis_at), (parts,), jnp.float32, low / len(pieces), top_value / len(pieces))
        gain = gain * jnp.repeat(jnp.exp(draws), dims[axis_at] // parts).reshape((-1,) + (1,) * (len(dims) - 1 - axis_at))
    return gain


def noise(rng, shape, width, limit, split=(), dtype=jnp.bfloat16):
    result = width * jax.random.normal(rng, shape, jnp.float32)
    if split:
        result = result * shard_levels(rng, shape, split, -0.22, 0.18)
    return jnp.clip(result, -limit, limit).astype(dtype)


def setup_inputs(seed: int = 0) -> dict:
    arg_keys = jax.random.split(jax.random.key(seed), 5)
    return {
        "image_in": noise(arg_keys[0], (HEIGHT, WIDTH, C), 1.0, 6.0, ((0, 4), (2, 4)), jnp.float32),
        "first_weight": noise(arg_keys[1], (3, 3, C, C), (9 * C) ** -0.5, 0.046875, ((2, 4), (3, 2)), jnp.float32),
        "second_weight": noise(arg_keys[2], (3, 3, C, C), (9 * C) ** -0.5, 0.046875, ((2, 2), (3, 4)), jnp.float32),
        "out_grad": noise(arg_keys[3], (HEIGHT, WIDTH, C), (1.0 / (ROWS_DEV * N_SLAB * WIDTH) ** 0.5), 0.13258252, ((0, 4), (2, 4)), jnp.float32),
    }


def conv_taps(padded, weight, row_count, col_count):
    summed = jnp.zeros((row_count * col_count, weight.shape[3]), jnp.float32)
    for row_off in range(3):
        for col_off in range(3):
            window = padded[row_off:row_off + row_count, col_off:col_off + col_count, :].reshape(row_count * col_count, -1)
            summed = summed + jnp.dot(window, weight[row_off, col_off], precision=lax.Precision.HIGHEST, preferred_element_type=jnp.float32)
    return summed.reshape(row_count, col_count, -1)


def reference(image_in, first_weight, second_weight, out_grad):
    row_count = image_in.shape[0]
    col_count = image_in.shape[1]
    padded = jnp.pad(image_in, ((1, 1), (1, 1), (0, 0)))
    hidden = jax.nn.silu(conv_taps(padded, first_weight, row_count, col_count))
    hidden_pad = jnp.pad(hidden, ((1, 1), (1, 1), (0, 0)))
    output = conv_taps(hidden_pad, second_weight, row_count, col_count)
    flat_grad = out_grad.reshape(row_count * col_count, -1)
    grads = []
    for row_off in range(3):
        for col_off in range(3):
            window = hidden_pad[row_off:row_off + row_count, col_off:col_off + col_count, :].reshape(row_count * col_count, -1)
            grads.append(lax.dot_general(window, flat_grad, (((0,), (0,)), ((), ())), precision=lax.Precision.HIGHEST, preferred_element_type=jnp.float32))
    weight_grad = jnp.stack(grads).reshape(3, 3, hidden.shape[2], flat_grad.shape[1])
    return output, weight_grad
```

```python
import jax
import jax.numpy as jnp
from jax import lax
from jax.sharding import PartitionSpec as P


def padded_cells(cells):
    return jnp.pad(cells, ((1, 1), (1, 1), (0, 0)))


def conv(padded, weight):
    return lax.conv_general_dilated(
        padded[None],
        weight,
        (1, 1),
        "VALID",
        dimension_numbers=("NHWC", "HWIO", "NHWC"),
        precision=lax.Precision.HIGH,
        preferred_element_type=jnp.float32,
    )[0]


def on_device(image_in, first_weight, second_weight, out_grad):
    slab = lax.axis_index("slab")
    block = first_weight.shape[3] // lax.axis_size("slab")
    first = lax.dynamic_slice_in_dim(first_weight, slab * block, block, axis=3)
    second = lax.dynamic_slice_in_dim(second_weight, slab * block, block, axis=2)
    image = lax.all_gather(image_in, "slab", axis=0, tiled=True)
    grad = lax.all_gather(out_grad, "slab", axis=0, tiled=True)
    rows, cols = image.shape[0], image.shape[1]
    hidden = jax.nn.silu(lax.psum(conv(padded_cells(image), first), "cin"))
    hidden_pad = padded_cells(hidden)
    part = conv(hidden_pad, second)
    part = lax.psum_scatter(part, "slab", scatter_dimension=0, tiled=True)
    output = lax.psum_scatter(part, "cout", scatter_dimension=1, tiled=True)
    flat_grad = grad.reshape(rows * cols, -1)
    grads = []
    for row_off in range(3):
        for col_off in range(3):
            window = hidden_pad[
                row_off : row_off + rows, col_off : col_off + cols, :
            ].reshape(rows * cols, -1)
            grads.append(
                lax.dot_general(
                    window,
                    flat_grad,
                    (((0,), (0,)), ((), ())),
                    precision=lax.Precision.HIGH,
                    preferred_element_type=jnp.float32,
                )
            )
    weight_grad = jnp.stack(grads).reshape(3, 3, block, flat_grad.shape[1])
    return (output, weight_grad)


def solution(mesh):
    in_specs = (
        P("slab", None, "cin"),
        P(None, None, "cin", "cout"),
        P(None, None, "cout", "cin"),
        P("slab", None, "cin"),
    )
    out_specs = (P("slab", "cout", "cin"), P(None, None, ("cout", "slab"), "cin"))
    return jax.shard_map(
        on_device, mesh=mesh, in_specs=in_specs, out_specs=out_specs, check_vma=False
    )
```

```python
import functools

import jax
import jax.numpy as jnp
from jax import lax
from jax.experimental import pallas as pl
from jax.experimental.pallas import tpu as pltpu
from jax.sharding import PartitionSpec as P

MESH = pl.DeviceIdType.MESH
F32, BF16 = jnp.float32, jnp.bfloat16


def split(value):
    high = value.astype(BF16)
    return high, (value - high.astype(F32)).astype(BF16)


def dot3(a_hi, a_lo, b_hi, b_lo):
    dot = functools.partial(jnp.dot, preferred_element_type=F32)
    return dot(a_hi, b_hi) + dot(a_lo, b_hi) + dot(a_hi, b_lo)


def shifted(value, width, axis):
    size = value.shape[axis]
    col = lax.rem(lax.broadcasted_iota(jnp.int32, value.shape, axis), width)
    before = jnp.where(col == 0, 0.0, pltpu.roll(value, 1, axis))
    after = jnp.where(col == width - 1, 0.0, pltpu.roll(value, size - 1, axis))
    return before, after


def kernel(
    rows, width, nz,
    image, w1, w2, grad,
    out_ref, wg,
    land, gland, halo, x_hi, x_lo, g_hi, g_lo,
    w1_stage, w2_stage, w1_hi, w1_lo, w2_hi, w2_lo,
    part, from_left, from_right, hid, h_hi, h_lo, ht_hi, ht_lo,
    outp, core_buf, y_buf, x_buf,
    local_sem, halo_s, halo_r, gat_s, gat_r, rs_s, rs_r, ag_s, ag_r, out_s, out_r,
):
    s, y, k = lax.axis_index("slab"), lax.axis_index("cout"), lax.axis_index("cin")
    pair = s // 2
    partner = s + 1 - 2 * lax.rem(s, 2)
    across = s + 2 - 4 * pair
    diagonal = partner + 2 - 4 * pair
    y_other = 1 - y
    order = [s, partner, 2 - pair, 3 - 3 * pair]
    block = w1_hi.shape[2]
    px = rows * width
    total_px = 4 * px
    shard = px // nz
    half = width // 2

    def remote(src, dst, send, recv, **dev):
        return pltpu.make_async_remote_copy(
            src_ref=src, dst_ref=dst, send_sem=send, recv_sem=recv,
            device_id=dev, device_id_type=MESH,
        )

    barrier = pltpu.get_barrier_semaphore()
    for other in (partner, across, diagonal):
        pl.semaphore_signal(barrier, inc=1, device_id={"slab": other}, device_id_type=MESH)
    pl.semaphore_signal(barrier, inc=1, device_id={"cout": y_other}, device_id_type=MESH)

    @pl.when(k > 0)
    def _():
        pl.semaphore_signal(barrier, inc=1, device_id={"cin": k - 1}, device_id_type=MESH)

    @pl.when(k < nz - 1)
    def _():
        pl.semaphore_signal(barrier, inc=1, device_id={"cin": k + 1}, device_id_type=MESH)

    own_copy = pltpu.make_async_copy(image, land.at[s], local_sem.at[0])
    own_copy.start()
    own_grad = pltpu.make_async_copy(grad, gland.at[s], local_sem.at[1])
    own_grad.start()

    def w1_copy(i):
        cols = pl.ds(pl.multiple_of(s * block, 128), block)
        return pltpu.make_async_copy(
            w1.at[pl.ds(3 * i, 3), :, cols], w1_stage.at[i % 2], local_sem.at[2 + i % 2]
        )

    def w2_copy(i):
        lines = pl.ds(pl.multiple_of(s * block, 128), block)
        return pltpu.make_async_copy(
            w2.at[pl.ds(3 * i, 3), lines, :], w2_stage, local_sem.at[4]
        )

    w1_copy(0).start()
    w1_copy(1).start()
    w2_copy(0).start()

    @pl.when(jnp.logical_and(k > 0, k < nz - 1))
    def _():
        pl.semaphore_wait(barrier, 6)

    @pl.when(jnp.logical_or(k == 0, k == nz - 1))
    def _():
        pl.semaphore_wait(barrier, 5)

    def halo_copies():
        edge = pl.ds(pl.multiple_of((1 - pair) * (px - width), 16), width)
        return [
            remote(image.at[edge, :], halo, halo_s.at[i], halo_r.at[0], slab=other)
            for i, other in enumerate((across, diagonal))
        ]

    faces = jnp.logical_or(s == 1, s == 2)

    @pl.when(faces)
    def _():
        for copy in halo_copies():
            copy.start()

    def gather(src, slots, base):
        near = remote(src, slots.at[s], gat_s.at[base], gat_r.at[base], slab=partner)
        far = remote(src, slots.at[s], gat_s.at[base + 1], gat_r.at[base + 1], slab=across)
        forward = remote(
            slots.at[across], slots.at[across], gat_s.at[base + 2], gat_r.at[base + 2],
            slab=partner,
        )
        return near, far, forward

    i_near, i_far, i_fwd = gather(image, land, 0)
    g_near, g_far, g_fwd = gather(grad, gland, 3)
    i_near.start()
    i_far.start()

    def split_rows(src, hi, lo, base, count):
        step = 64

        @pl.loop(0, count // step)
        def _(i):
            at = pl.ds(pl.multiple_of(i * step, step), step)
            to = pl.ds(pl.multiple_of(base + i * step, 64), step)
            high, low = split(src[at, :])
            hi[to, :] = high
            lo[to, :] = low

    def split_taps(stage, hi, lo, base):
        step = 64
        lines = stage.shape[1]

        @pl.loop(0, 3)
        def _(t):
            @pl.loop(0, lines // step)
            def _(i):
                at = pl.ds(pl.multiple_of(i * step, step), step)
                high, low = split(stage[t, at, :])
                hi[base + t, at, :] = high
                lo[base + t, at, :] = low

    for ref in (x_hi, x_lo, g_hi, g_lo):
        zero = jnp.zeros((width, ref.shape[1]), BF16)
        ref[0:width, :] = zero
        ref[total_px + width : total_px + 2 * width, :] = zero

    for i in range(3):
        w1_copy(i).wait()
        split_taps(w1_stage.at[i % 2], w1_hi, w1_lo, 3 * i)
        if i == 0:
            w1_copy(2).start()

    own_copy.wait()
    split_rows(land.at[s], x_hi, x_lo, width + s * px, px)
    i_near.wait_recv()
    split_rows(land.at[partner], x_hi, x_lo, width + partner * px, px)
    halo_copies()[0].wait_recv()
    split_rows(halo, x_hi, x_lo, width + (1 - pair) * 2 * px + pair * (2 * px - width), width)

    def conv1(c):
        tile = px // 2
        per = tile // shard

        @pl.loop(0, 2)
        def _(m):
            def taps(b):
                total = None
                for a in range(3):
                    at = pl.ds(
                        pl.multiple_of(order[c] * px + m * tile + a * width, 64), tile
                    )
                    term = dot3(
                        x_hi[at, :], x_lo[at, :], w1_hi[3 * a + b], w1_lo[3 * a + b]
                    )
                    total = term if total is None else total + term
                return total

            value = taps(1)
            value = value + shifted(taps(0), width, 0)[0]
            value = value + shifted(taps(2), width, 0)[1]
            part[c, pl.ds(m * per, per)] = value.reshape(per, shard, block)

    def rs_right(c, j, src):
        return remote(src, from_left.at[c, j], rs_s.at[0, c, j], rs_r.at[0, c, j], cin=k + 1)

    def rs_left(c, j, src):
        return remote(src, from_right.at[c, j], rs_s.at[1, c, j], rs_r.at[1, c, j], cin=k - 1)

    def rs_stage(c, m):
        @pl.when(k == m)
        def _():
            for j in range(nz - 1, m, -1):
                if m == 0:
                    rs_right(c, j, part.at[c, j]).start()
                else:
                    rs_right(c, j, from_left.at[c, j]).wait_recv()
                    from_left[c, j] = from_left[c, j] + part[c, j]
                    rs_right(c, j, from_left.at[c, j]).start()

        @pl.when(k == nz - 1 - m)
        def _():
            for j in range(nz - 1 - m):
                if m == 0:
                    rs_left(c, j, part.at[c, j]).start()
                else:
                    rs_left(c, j, from_right.at[c, j]).wait_recv()
                    from_right[c, j] = from_right[c, j] + part[c, j]
                    rs_left(c, j, from_right.at[c, j]).start()

    def ag_right(c, j):
        return remote(hid.at[c, j], hid.at[c, j], ag_s.at[0, c, j], ag_r.at[c, j], cin=k + 1)

    def ag_left(c, j):
        return remote(hid.at[c, j], hid.at[c, j], ag_s.at[1, c, j], ag_r.at[c, j], cin=k - 1)

    def rs_final(c):
        @pl.when(k > 0)
        def _():
            rs_right(c, k, part.at[c, k]).wait_recv()
            part[c, k] = part[c, k] + from_left[c, k]

        @pl.when(k < nz - 1)
        def _():
            rs_left(c, k, part.at[c, k]).wait_recv()
            part[c, k] = part[c, k] + from_right[c, k]

        hid[c, k] = jax.nn.silu(part[c, k])

        @pl.when(k < nz - 1)
        def _():
            ag_right(c, k).start()

        @pl.when(k > 0)
        def _():
            ag_left(c, k).start()

    def ag_stage(c, m):
        @pl.when(jnp.logical_and(k >= m, k < nz - 1))
        def _():
            ag_right(c, k - m).wait_recv()
            ag_right(c, k - m).start()

        @pl.when(jnp.logical_and(k + m <= nz - 1, k > 0))
        def _():
            ag_left(c, k + m).wait_recv()
            ag_left(c, k + m).start()

    def ag_final(c):
        @pl.when(k == nz - 1)
        def _():
            for j in range(nz - 1):
                ag_right(c, j).wait_recv()

        @pl.when(k == 0)
        def _():
            for j in range(1, nz):
                ag_left(c, j).wait_recv()

    def conv2(c):
        value = hid[c].reshape(px, block)
        before, after = shifted(value, width, 0)
        for b, item in enumerate((before, value, after)):
            high, low = split(item)
            h_hi[:, b * block : (b + 1) * block] = high
            h_lo[:, b * block : (b + 1) * block] = low
        tile = px // 2
        lines = tile // width

        @pl.loop(0, 6)
        def _(i):
            m, a = i // 3, lax.rem(i, 3)
            at = pl.ds(pl.multiple_of(m * tile, tile), tile)
            to = pl.ds(order[c] * rows + m * lines + 2 - a, lines)
            term = dot3(h_hi[at, :], h_lo[at, :], w2_hi[a], w2_lo[a])
            outp[to] = outp[to] + term.reshape(lines, width, -1)

    def wgrad(c, first):
        value = hid[c].reshape(px, block).T
        before, after = shifted(value, width, 1)
        for b, item in enumerate((before, value, after)):
            high, low = split(item)
            ht_hi[b] = high
            ht_lo[b] = low

        @pl.loop(0, 9)
        def _(i):
            a, b = i // 3, lax.rem(i, 3)
            at = pl.ds(pl.multiple_of(order[c] * px + (2 - a) * width, 64), px)
            term = dot3(ht_hi[b], ht_lo[b], g_hi[at, :], g_lo[at, :])
            wg[i] = term if first else wg[i] + term

    def out_core(i, slab):
        return remote(
            outp.at[pl.ds(slab * rows + 1, rows)], core_buf.at[i],
            out_s.at[i], out_r.at[i], slab=partner,
        )

    def col(which):
        return pl.ds(pl.multiple_of(which * half, 8), half)

    def out_y(i):
        return remote(
            core_buf.at[i, :, col(y_other), :], y_buf.at[i],
            out_s.at[2 + i], out_r.at[2 + i], cout=y_other,
        )

    def add_core(i, slab):
        @pl.loop(0, rows)
        def _(r):
            core_buf[i, r] = core_buf[i, r] + outp[slab * rows + 1 + r]

    def add_y(i):
        @pl.loop(0, rows)
        def _(r):
            y_buf[i, r] = y_buf[i, r] + core_buf[i, r, col(y), :]

    out_x = remote(y_buf.at[1], x_buf, out_s.at[4], out_r.at[4], slab=across)

    conv1(0)
    rs_stage(0, 0)
    g_near.start()
    conv1(1)
    rs_stage(1, 0)
    for m in range(1, nz - 1):
        rs_stage(0, m)
    i_far.wait_recv()
    i_fwd.start()
    g_far.start()
    split_rows(land.at[across], x_hi, x_lo, width + across * px, px)
    i_fwd.wait_recv()
    split_rows(land.at[diagonal], x_hi, x_lo, width + diagonal * px, px)
    rs_final(0)
    for m in range(1, nz - 1):
        rs_stage(1, m)
    conv1(2)
    rs_stage(2, 0)
    rs_final(1)
    for m in range(1, nz - 1):
        ag_stage(0, m)
    conv1(3)
    rs_stage(3, 0)
    for m in range(1, nz - 1):
        rs_stage(2, m)
    for m in range(1, nz - 1):
        ag_stage(1, m)

    for i in range(3):
        w2_copy(i).wait()
        lines = block

        @pl.loop(0, 9 if False else 3)
        def _(t):
            step = 64

            @pl.loop(0, lines // step)
            def _(n):
                at = pl.ds(pl.multiple_of(n * step, step), step)
                to = pl.ds(pl.multiple_of(t * lines + n * step, step), step)
                high, low = split(w2_stage[t, at, :])
                w2_hi[i, to, :] = high
                w2_lo[i, to, :] = low

        if i < 2:
            w2_copy(i + 1).start()
    outp[...] = jnp.zeros_like(outp)

    ag_final(0)
    conv2(0)
    rs_final(2)
    for m in range(1, nz - 1):
        rs_stage(3, m)
    ag_final(1)
    conv2(1)
    for m in range(1, nz - 1):
        ag_stage(2, m)
    rs_final(3)

    own_grad.wait()
    split_rows(gland.at[s], g_hi, g_lo, width + s * px, px)
    g_near.wait_recv()
    split_rows(gland.at[partner], g_hi, g_lo, width + partner * px, px)
    g_far.wait_recv()
    g_fwd.start()
    split_rows(gland.at[across], g_hi, g_lo, width + across * px, px)
    g_fwd.wait_recv()
    split_rows(gland.at[diagonal], g_hi, g_lo, width + diagonal * px, px)

    ag_final(2)
    conv2(2)
    out_core(0, partner).start()
    for m in range(1, nz - 1):
        ag_stage(3, m)
    wgrad(0, True)
    out_core(0, partner).wait_recv()
    add_core(0, s)
    out_y(0).start()
    ag_final(3)
    conv2(3)
    out_core(1, diagonal).start()
    wgrad(1, False)
    out_core(1, diagonal).wait_recv()
    add_core(1, across)
    out_y(1).start()
    wgrad(2, False)
    out_y(0).wait_recv()
    add_y(0)
    out_y(1).wait_recv()
    add_y(1)
    out_x.start()
    wgrad(3, False)
    out_x.wait_recv()
    out_ref[...] = y_buf[0] + x_buf[...]

    @pl.when(faces)
    def _():
        for copy in halo_copies():
            copy.wait_send()

    for copy in (i_near, i_far, i_fwd, g_near, g_far, g_fwd):
        copy.wait_send()
    for c in range(4):
        for j in range(nz):
            @pl.when(k < j)
            def _():
                rs_right(c, j, part.at[c, j]).wait_send()

            @pl.when(k > j)
            def _():
                rs_left(c, j, part.at[c, j]).wait_send()

            @pl.when(jnp.logical_and(k >= j, k < nz - 1))
            def _():
                ag_right(c, j).wait_send()

            @pl.when(jnp.logical_and(k <= j, k > 0))
            def _():
                ag_left(c, j).wait_send()
    for i, slab in enumerate((partner, diagonal)):
        out_core(i, slab).wait_send()
        out_y(i).wait_send()
    out_x.wait_send()


def fused(image_in, first_weight, second_weight, out_grad):
    rows, width, depth = image_in.shape
    nz = lax.axis_size("cin")
    px = rows * width
    block = first_weight.shape[3] // 4
    cols = second_weight.shape[3]
    shard = px // nz
    tall = 4 * px + 2 * width
    dma = pltpu.SemaphoreType.DMA
    vm = pltpu.VMEM
    scratch = [
        vm((4, px, depth), F32), vm((4, px, cols), F32), vm((width, depth), F32),
        vm((tall, depth), BF16), vm((tall, depth), BF16),
        vm((tall, cols), BF16), vm((tall, cols), BF16),
        vm((2, 3, depth, block), F32), vm((3, block, cols), F32),
        vm((9, depth, block), BF16), vm((9, depth, block), BF16),
        vm((3, 3 * block, cols), BF16), vm((3, 3 * block, cols), BF16),
        vm((4, nz, shard, block), F32), vm((4, nz, shard, block), F32),
        vm((4, nz, shard, block), F32), vm((4, nz, shard, block), F32),
        vm((px, 3 * block), BF16), vm((px, 3 * block), BF16),
        vm((3, block, px), BF16), vm((3, block, px), BF16),
        vm((4 * rows + 2, width, cols), F32),
        vm((2, rows, width, cols), F32), vm((2, rows, width // 2, cols), F32),
        vm((rows, width // 2, cols), F32),
        dma((5,)), dma((2,)), dma((1,)), dma((6,)), dma((6,)),
        dma((2, 4, nz)), dma((2, 4, nz)), dma((2, 4, nz)), dma((4, nz)),
        dma((5,)), dma((5,)),
    ]
    any_spec = pl.BlockSpec(memory_space=pl.ANY)
    vmem_spec = pl.BlockSpec(memory_space=pltpu.VMEM)
    output, weight_grad = pl.pallas_call(
        functools.partial(kernel, rows, width, nz),
        out_shape=(
            jax.ShapeDtypeStruct((rows, width // 2, cols), F32),
            jax.ShapeDtypeStruct((9, block, cols), F32),
        ),
        in_specs=[any_spec] * 4,
        out_specs=(vmem_spec, vmem_spec),
        scratch_shapes=scratch,
        compiler_params=pltpu.CompilerParams(
            collective_id=0, has_side_effects=True, vmem_limit_bytes=63 * 1024 * 1024
        ),
        cost_estimate=pl.CostEstimate(
            flops=3 * 6 * 9 * 4 * px * block * depth,
            bytes_accessed=4 * (18 * block * depth + 9 * block * cols),
            transcendentals=4 * px * block,
        ),
    )(
        image_in.reshape(px, depth),
        first_weight.reshape(9, depth, -1),
        second_weight.reshape(9, -1, cols),
        out_grad.reshape(px, cols),
    )
    return output, weight_grad.reshape(3, 3, block, cols)


def fits(image_in, first_weight, second_weight):
    rows, width, depth = image_in.shape
    nz = lax.axis_size("cin")
    return (
        lax.axis_size("slab") == 4
        and lax.axis_size("cout") == 2
        and nz >= 2
        and nz % 2 == 0
        and rows % 2 == 0
        and width % 64 == 0
        and (rows * width) % (8 * nz) == 0
        and depth % 128 == 0
        and first_weight.shape[3] % 512 == 0
        and second_weight.shape[3] % 128 == 0
        and depth <= 512
        and second_weight.shape[3] <= 512
        and first_weight.shape[3] <= 1024
        and rows * width <= 512
    )


def padded_cells(cells):
    return jnp.pad(cells, ((1, 1), (1, 1), (0, 0)))


def conv(padded, weight):
    return lax.conv_general_dilated(
        padded[None],
        weight,
        (1, 1),
        "VALID",
        dimension_numbers=("NHWC", "HWIO", "NHWC"),
        precision=lax.Precision.HIGH,
        preferred_element_type=jnp.float32,
    )[0]


def on_device(image_in, first_weight, second_weight, out_grad):
    if fits(image_in, first_weight, second_weight):
        return fused(image_in, first_weight, second_weight, out_grad)
    slab = lax.axis_index("slab")
    block = first_weight.shape[3] // lax.axis_size("slab")
    first = lax.dynamic_slice_in_dim(first_weight, slab * block, block, axis=3)
    second = lax.dynamic_slice_in_dim(second_weight, slab * block, block, axis=2)
    image = lax.all_gather(image_in, "slab", axis=0, tiled=True)
    grad = lax.all_gather(out_grad, "slab", axis=0, tiled=True)
    rows, cols = image.shape[0], image.shape[1]
    hidden = jax.nn.silu(lax.psum(conv(padded_cells(image), first), "cin"))
    hidden_pad = padded_cells(hidden)
    part = conv(hidden_pad, second)
    part = lax.psum_scatter(part, "slab", scatter_dimension=0, tiled=True)
    output = lax.psum_scatter(part, "cout", scatter_dimension=1, tiled=True)
    flat_grad = grad.reshape(rows * cols, -1)
    grads = []
    for row_off in range(3):
        for col_off in range(3):
            window = hidden_pad[
                row_off : row_off + rows, col_off : col_off + cols, :
            ].reshape(rows * cols, -1)
            grads.append(
                lax.dot_general(
                    window,
                    flat_grad,
                    (((0,), (0,)), ((), ())),
                    precision=lax.Precision.HIGH,
                    preferred_element_type=jnp.float32,
                )
            )
    weight_grad = jnp.stack(grads).reshape(3, 3, block, flat_grad.shape[1])
    return (output, weight_grad)


def solution(mesh):
    in_specs = (
        P("slab", None, "cin"),
        P(None, None, "cin", "cout"),
        P(None, None, "cout", "cin"),
        P("slab", None, "cin"),
    )
    out_specs = (P("slab", "cout", "cin"), P(None, None, ("cout", "slab"), "cin"))
    return jax.shard_map(
        on_device, mesh=mesh, in_specs=in_specs, out_specs=out_specs, check_vma=False
    )
```

```python
import functools

import jax
import jax.numpy as jnp
from jax import lax
from jax.experimental import pallas as pl
from jax.experimental.pallas import tpu as pltpu
from jax.sharding import PartitionSpec as P

MESH = pl.DeviceIdType.MESH
F32, BF16 = jnp.float32, jnp.bfloat16


def split(value):
    high = value.astype(BF16)
    return high, (value - high.astype(F32)).astype(BF16)


def dot3(a_hi, a_lo, b_hi, b_lo):
    dot = functools.partial(jnp.dot, preferred_element_type=F32)
    return dot(a_hi, b_hi) + dot(a_lo, b_hi) + dot(a_hi, b_lo)


def shifted(value, width, axis):
    size = value.shape[axis]
    col = lax.rem(lax.broadcasted_iota(jnp.int32, value.shape, axis), width)
    before = jnp.where(col == 0, 0.0, pltpu.roll(value, 1, axis))
    after = jnp.where(col == width - 1, 0.0, pltpu.roll(value, size - 1, axis))
    return before, after


def kernel(
    rows, width, nz,
    image, w1, w2, grad,
    out_ref, wg,
    land, gland, halo, ghalo, x_hi, x_lo, g_hi, g_lo,
    w1_stage, w2_stage, w1_hi, w1_lo, w2_hi, w2_lo,
    part, from_left, from_right, hid, h_hi, h_lo, ht_hi, ht_lo,
    outp, core_buf, y_buf, x_buf,
    local_sem, halo_s, halo_r, gat_s, gat_r, rs_s, rs_r, ag_s, ag_r, out_s, out_r,
):
    s, y, k = lax.axis_index("slab"), lax.axis_index("cout"), lax.axis_index("cin")
    pair = s // 2
    partner = s + 1 - 2 * lax.rem(s, 2)
    across = s + 2 - 4 * pair
    diagonal = partner + 2 - 4 * pair
    y_other = 1 - y
    order = [s, partner, 2 - pair, 3 - 3 * pair]
    block = w1_hi.shape[2]
    px = rows * width
    total_px = 4 * px
    shard = px // nz
    half = width // 2

    def remote(src, dst, send, recv, **dev):
        return pltpu.make_async_remote_copy(
            src_ref=src, dst_ref=dst, send_sem=send, recv_sem=recv,
            device_id=dev, device_id_type=MESH,
        )

    barrier = pltpu.get_barrier_semaphore()
    for other in (partner, across, diagonal):
        pl.semaphore_signal(barrier, inc=1, device_id={"slab": other}, device_id_type=MESH)
    pl.semaphore_signal(barrier, inc=1, device_id={"cout": y_other}, device_id_type=MESH)

    @pl.when(k > 0)
    def _():
        pl.semaphore_signal(barrier, inc=1, device_id={"cin": k - 1}, device_id_type=MESH)

    @pl.when(k < nz - 1)
    def _():
        pl.semaphore_signal(barrier, inc=1, device_id={"cin": k + 1}, device_id_type=MESH)

    own_copy = pltpu.make_async_copy(image, land.at[s], local_sem.at[0])
    own_copy.start()
    own_grad = pltpu.make_async_copy(grad, gland.at[s], local_sem.at[1])
    own_grad.start()

    def w1_copy(i):
        cols = pl.ds(pl.multiple_of(s * block, 128), block)
        return pltpu.make_async_copy(
            w1.at[pl.ds(3 * i, 3), :, cols], w1_stage.at[i % 2], local_sem.at[2 + i % 2]
        )

    def w2_copy(i):
        lines = pl.ds(pl.multiple_of(s * block, 128), block)
        return pltpu.make_async_copy(
            w2.at[pl.ds(3 * i, 3), lines, :], w2_stage, local_sem.at[4]
        )

    w1_copy(0).start()
    w1_copy(1).start()
    w2_copy(0).start()

    @pl.when(jnp.logical_and(k > 0, k < nz - 1))
    def _():
        pl.semaphore_wait(barrier, 6)

    @pl.when(jnp.logical_or(k == 0, k == nz - 1))
    def _():
        pl.semaphore_wait(barrier, 5)

    def halo_copies(n):
        edge = pl.ds(pl.multiple_of((1 - pair) * (px - width), 16), width)
        src, dst = ((image, halo), (grad, ghalo))[n]
        return [
            remote(src.at[edge, :], dst, halo_s.at[n, i], halo_r.at[n], slab=other)
            for i, other in enumerate((across, diagonal))
        ]

    faces = jnp.logical_or(s == 1, s == 2)

    @pl.when(faces)
    def _():
        for copy in halo_copies(0):
            copy.start()

    def gather(src, slots, base):
        near = remote(src, slots.at[s], gat_s.at[base], gat_r.at[base], slab=partner)
        far = remote(src, slots.at[s], gat_s.at[base + 1], gat_r.at[base + 1], slab=across)
        forward = remote(
            slots.at[across], slots.at[across], gat_s.at[base + 2], gat_r.at[base + 2],
            slab=partner,
        )
        return near, far, forward

    i_near, i_far, i_fwd = gather(image, land, 0)
    g_near, g_far, g_fwd = gather(grad, gland, 3)
    i_near.start()
    i_far.start()

    def split_rows(src, hi, lo, base, count):
        step = 64

        @pl.loop(0, count // step)
        def _(i):
            at = pl.ds(pl.multiple_of(i * step, step), step)
            to = pl.ds(pl.multiple_of(base + i * step, 64), step)
            high, low = split(src[at, :])
            hi[to, :] = high
            lo[to, :] = low

    def split_taps(stage, hi, lo, base):
        step = 64
        lines = stage.shape[1]

        @pl.loop(0, 3)
        def _(t):
            @pl.loop(0, lines // step)
            def _(i):
                at = pl.ds(pl.multiple_of(i * step, step), step)
                high, low = split(stage[t, at, :])
                hi[base + t, at, :] = high
                lo[base + t, at, :] = low

    def split_w2(i):
        w2_copy(i).wait()
        step = 64

        @pl.loop(0, 3)
        def _(t):
            @pl.loop(0, block // step)
            def _(n):
                at = pl.ds(pl.multiple_of(n * step, step), step)
                to = pl.ds(pl.multiple_of(t * block + n * step, step), step)
                high, low = split(w2_stage[t, at, :])
                w2_hi[i, to, :] = high
                w2_lo[i, to, :] = low

        if i < 2:
            w2_copy(i + 1).start()

    for ref in (x_hi, x_lo, g_hi, g_lo):
        zero = jnp.zeros((width, ref.shape[1]), BF16)
        ref[0:width, :] = zero
        ref[total_px + width : total_px + 2 * width, :] = zero

    for i in range(3):
        w1_copy(i).wait()
        split_taps(w1_stage.at[i % 2], w1_hi, w1_lo, 3 * i)
        if i == 0:
            w1_copy(2).start()

    own_copy.wait()
    split_rows(land.at[s], x_hi, x_lo, width + s * px, px)
    i_near.wait_recv()
    split_rows(land.at[partner], x_hi, x_lo, width + partner * px, px)
    edge_row = width + (1 - pair) * 2 * px + pair * (2 * px - width)
    halo_copies(0)[0].wait_recv()
    split_rows(halo, x_hi, x_lo, edge_row, width)

    def conv1(c, m):
        tile = px // 2
        per = tile // shard

        def taps(b):
            total = None
            for a in range(3):
                at = pl.ds(
                    pl.multiple_of(order[c] * px + m * tile + a * width, 64), tile
                )
                term = dot3(
                    x_hi[at, :], x_lo[at, :], w1_hi[3 * a + b], w1_lo[3 * a + b]
                )
                total = term if total is None else total + term
            return total

        value = taps(1)
        value = value + shifted(taps(0), width, 0)[0]
        value = value + shifted(taps(2), width, 0)[1]
        part[c, pl.ds(m * per, per)] = value.reshape(per, shard, block)

    def rs_right(c, j, src):
        return remote(src, from_left.at[c, j], rs_s.at[0, c, j], rs_r.at[0, c, j], cin=k + 1)

    def rs_left(c, j, src):
        return remote(src, from_right.at[c, j], rs_s.at[1, c, j], rs_r.at[1, c, j], cin=k - 1)

    def rs_stage(c, m, i):
        @pl.when(k == m)
        def _():
            j = nz - 1 - i
            if m > 0:
                rs_right(c, j, from_left.at[c, j]).wait_recv()
                from_left[c, j] = from_left[c, j] + part[c, j]
                rs_right(c, j, from_left.at[c, j]).start()
            else:
                rs_right(c, j, part.at[c, j]).start()

        @pl.when(k == nz - 1 - m)
        def _():
            if m > 0:
                rs_left(c, i, from_right.at[c, i]).wait_recv()
                from_right[c, i] = from_right[c, i] + part[c, i]
                rs_left(c, i, from_right.at[c, i]).start()
            else:
                rs_left(c, i, part.at[c, i]).start()

    def ag_right(c, j):
        return remote(hid.at[c, j], hid.at[c, j], ag_s.at[0, c, j], ag_r.at[c, j], cin=k + 1)

    def ag_left(c, j):
        return remote(hid.at[c, j], hid.at[c, j], ag_s.at[1, c, j], ag_r.at[c, j], cin=k - 1)

    def rs_final(c):
        @pl.when(k > 0)
        def _():
            rs_right(c, k, part.at[c, k]).wait_recv()
            part[c, k] = part[c, k] + from_left[c, k]

        @pl.when(k < nz - 1)
        def _():
            rs_left(c, k, part.at[c, k]).wait_recv()
            part[c, k] = part[c, k] + from_right[c, k]

        hid[c, k] = jax.nn.silu(part[c, k])

        @pl.when(k < nz - 1)
        def _():
            ag_right(c, k).start()

        @pl.when(k > 0)
        def _():
            ag_left(c, k).start()

    def ag_stage(c, m):
        @pl.when(jnp.logical_and(k >= m, k < nz - 1))
        def _():
            ag_right(c, k - m).wait_recv()
            ag_right(c, k - m).start()

        @pl.when(jnp.logical_and(k + m <= nz - 1, k > 0))
        def _():
            ag_left(c, k + m).wait_recv()
            ag_left(c, k + m).start()

    def ag_final(c):
        @pl.when(k == nz - 1)
        def _():
            for j in range(nz - 1):
                ag_right(c, j).wait_recv()

        @pl.when(k == 0)
        def _():
            for j in range(1, nz):
                ag_left(c, j).wait_recv()

    def conv2_start(c):
        value = hid[c].reshape(px, block)
        before, after = shifted(value, width, 0)
        for b, item in enumerate((before, value, after)):
            high, low = split(item)
            h_hi[:, b * block : (b + 1) * block] = high
            h_lo[:, b * block : (b + 1) * block] = low

    def conv2(c, m):
        tile = px // 2
        lines = tile // width

        @pl.loop(0, 3)
        def _(a):
            at = slice(m * tile, (m + 1) * tile)
            to = pl.ds(order[c] * rows + m * lines + 2 - a, lines)
            term = dot3(h_hi[at, :], h_lo[at, :], w2_hi[a], w2_lo[a])
            outp[to] = outp[to] + term.reshape(lines, width, -1)

    def wgrad_start(c):
        value = hid[c].reshape(px, block).T
        before, after = shifted(value, width, 1)
        for b, item in enumerate((before, value, after)):
            high, low = split(item)
            ht_hi[b] = high
            ht_lo[b] = low

    def wgrad(c, a):
        at = pl.ds(pl.multiple_of(order[c] * px + (2 - a) * width, 64), px)

        @pl.loop(0, 3)
        def _(b):
            term = dot3(ht_hi[b], ht_lo[b], g_hi[at, :], g_lo[at, :])
            wg[3 * a + b] = term if c == 0 else wg[3 * a + b] + term

    def out_core(i, slab):
        return remote(
            outp.at[pl.ds(slab * rows + 1, rows)], core_buf.at[i],
            out_s.at[i], out_r.at[i], slab=partner,
        )

    def col(which):
        return pl.ds(pl.multiple_of(which * half, 8), half)

    part_rows = rows // 2

    def out_y(i, h):
        at = pl.ds(h * part_rows, part_rows) if i else pl.ds(0, rows)
        return remote(
            core_buf.at[i, at, col(y_other), :], y_buf.at[i, at],
            out_s.at[2 + i + h], out_r.at[2 + i + h], cout=y_other,
        )

    def out_x(h):
        at = pl.ds(h * part_rows, part_rows)
        return remote(
            y_buf.at[1, at], x_buf.at[at], out_s.at[5 + h], out_r.at[5 + h], slab=across
        )

    def add_core(i, slab):
        @pl.loop(0, rows)
        def _(r):
            core_buf[i, r] = core_buf[i, r] + outp[slab * rows + 1 + r]

    def add_y(i, low, high):
        @pl.loop(low, high)
        def _(r):
            y_buf[i, r] = y_buf[i, r] + core_buf[i, r, col(y), :]

    steps = [[], [], [], []]
    for c in range(4):
        todo = [functools.partial(rs_stage, c, m, i) for m in range(1, nz - 1) for i in range(nz - 1 - m)]
        todo.append(functools.partial(rs_final, c))
        todo += [functools.partial(ag_stage, c, m) for m in range(1, nz - 1)]
        todo.append(functools.partial(ag_final, c))
        steps[c] = todo

    def advance(c, count=1):
        for _ in range(count):
            if steps[c]:
                steps[c].pop(0)()

    def send_sums(c):
        for i in range(nz - 1):
            rs_stage(c, 0, i)

    conv1(0, 0)
    conv1(0, 1)
    send_sums(0)
    conv1(1, 0)
    advance(0)
    conv1(1, 1)
    send_sums(1)
    advance(0)

    @pl.when(faces)
    def _():
        for copy in halo_copies(1):
            copy.start()

    g_near.start()
    split_w2(0)
    advance(0)
    split_w2(1)
    split_w2(2)
    advance(0)
    own_grad.wait()
    split_rows(gland.at[s], g_hi, g_lo, width + s * px, px)
    outp[...] = jnp.zeros_like(outp)
    advance(1)
    i_far.wait_recv()
    i_fwd.start()
    g_far.start()
    split_rows(land.at[across], x_hi, x_lo, width + across * px, px)
    i_fwd.wait_recv()
    split_rows(land.at[diagonal], x_hi, x_lo, width + diagonal * px, px)
    advance(0)
    conv1(2, 0)
    advance(0)
    advance(1)
    conv1(2, 1)
    send_sums(2)
    advance(1)
    conv1(3, 0)
    advance(1)
    conv1(3, 1)
    send_sums(3)
    advance(0, 99)
    conv2_start(0)
    conv2(0, 0)
    advance(1)
    conv2(0, 1)
    advance(1)
    g_near.wait_recv()
    split_rows(gland.at[partner], g_hi, g_lo, width + partner * px, px)
    halo_copies(1)[0].wait_recv()
    split_rows(ghalo, g_hi, g_lo, edge_row, width)
    wgrad_start(0)
    wgrad(0, 0)
    advance(1)
    advance(2)
    wgrad(0, 1)
    advance(2)
    wgrad(0, 2)
    advance(1, 99)
    conv2_start(1)
    conv2(1, 0)
    advance(2)
    conv2(1, 1)
    advance(2)
    wgrad_start(1)
    wgrad(1, 0)
    advance(2)
    advance(3)
    g_far.wait_recv()
    g_fwd.start()
    split_rows(gland.at[across], g_hi, g_lo, width + across * px, px)
    wgrad(1, 1)
    advance(3)
    wgrad(1, 2)
    advance(2)
    advance(3)
    g_fwd.wait_recv()
    split_rows(gland.at[diagonal], g_hi, g_lo, width + diagonal * px, px)
    advance(2, 99)
    conv2_start(2)
    conv2(2, 0)
    advance(3)
    conv2(2, 1)
    out_core(0, partner).start()
    advance(3)
    wgrad_start(2)
    wgrad(2, 0)
    advance(3)
    out_core(0, partner).wait_recv()
    add_core(0, s)
    out_y(0, 0).start()
    advance(3, 99)
    conv2_start(3)
    conv2(3, 0)
    conv2(3, 1)
    out_core(1, diagonal).start()
    wgrad(2, 1)
    out_core(1, diagonal).wait_recv()
    add_core(1, across)
    out_y(1, 0).start()
    out_y(1, 1).start()
    wgrad(2, 2)
    wgrad_start(3)
    out_y(1, 0).wait_recv()
    add_y(1, 0, part_rows)
    out_x(0).start()
    wgrad(3, 0)
    out_y(1, 1).wait_recv()
    add_y(1, part_rows, rows)
    out_x(1).start()
    wgrad(3, 1)
    out_y(0, 0).wait_recv()
    add_y(0, 0, rows)
    wgrad(3, 2)
    out_x(0).wait_recv()
    out_x(1).wait_recv()
    out_ref[...] = y_buf[0] + x_buf[...]

    @pl.when(faces)
    def _():
        for copy in halo_copies(0) + halo_copies(1):
            copy.wait_send()

    for copy in (i_near, i_far, i_fwd, g_near, g_far, g_fwd):
        copy.wait_send()
    for c in range(4):
        for j in range(nz):
            @pl.when(k < j)
            def _():
                rs_right(c, j, part.at[c, j]).wait_send()

            @pl.when(k > j)
            def _():
                rs_left(c, j, part.at[c, j]).wait_send()

            @pl.when(jnp.logical_and(k >= j, k < nz - 1))
            def _():
                ag_right(c, j).wait_send()

            @pl.when(jnp.logical_and(k <= j, k > 0))
            def _():
                ag_left(c, j).wait_send()
    for i, slab in enumerate((partner, diagonal)):
        out_core(i, slab).wait_send()
    for i, h in ((0, 0), (1, 0), (1, 1)):
        out_y(i, h).wait_send()
    for h in range(2):
        out_x(h).wait_send()


def fused(image_in, first_weight, second_weight, out_grad):
    rows, width, depth = image_in.shape
    nz = lax.axis_size("cin")
    px = rows * width
    block = first_weight.shape[3] // 4
    cols = second_weight.shape[3]
    shard = px // nz
    tall = 4 * px + 2 * width
    dma = pltpu.SemaphoreType.DMA
    vm = pltpu.VMEM
    scratch = [
        vm((4, px, depth), F32), vm((4, px, cols), F32), vm((width, depth), F32), vm((width, cols), F32),
        vm((tall, depth), BF16), vm((tall, depth), BF16),
        vm((tall, cols), BF16), vm((tall, cols), BF16),
        vm((2, 3, depth, block), F32), vm((3, block, cols), F32),
        vm((9, depth, block), BF16), vm((9, depth, block), BF16),
        vm((3, 3 * block, cols), BF16), vm((3, 3 * block, cols), BF16),
        vm((4, nz, shard, block), F32), vm((4, nz, shard, block), F32),
        vm((4, nz, shard, block), F32), vm((4, nz, shard, block), F32),
        vm((px, 3 * block), BF16), vm((px, 3 * block), BF16),
        vm((3, block, px), BF16), vm((3, block, px), BF16),
        vm((4 * rows + 2, width, cols), F32),
        vm((2, rows, width, cols), F32), vm((2, rows, width // 2, cols), F32),
        vm((rows, width // 2, cols), F32),
        dma((5,)), dma((2, 2)), dma((2,)), dma((6,)), dma((6,)),
        dma((2, 4, nz)), dma((2, 4, nz)), dma((2, 4, nz)), dma((4, nz)),
        dma((7,)), dma((7,)),
    ]
    any_spec = pl.BlockSpec(memory_space=pl.ANY)
    vmem_spec = pl.BlockSpec(memory_space=pltpu.VMEM)
    output, weight_grad = pl.pallas_call(
        functools.partial(kernel, rows, width, nz),
        out_shape=(
            jax.ShapeDtypeStruct((rows, width // 2, cols), F32),
            jax.ShapeDtypeStruct((9, block, cols), F32),
        ),
        in_specs=[any_spec] * 4,
        out_specs=(vmem_spec, vmem_spec),
        scratch_shapes=scratch,
        compiler_params=pltpu.CompilerParams(
            collective_id=0, has_side_effects=True, vmem_limit_bytes=63 * 1024 * 1024
        ),
        cost_estimate=pl.CostEstimate(
            flops=3 * 6 * 9 * 4 * px * block * depth,
            bytes_accessed=4 * (18 * block * depth + 9 * block * cols),
            transcendentals=4 * px * block,
        ),
    )(
        image_in.reshape(px, depth),
        first_weight.reshape(9, depth, -1),
        second_weight.reshape(9, -1, cols),
        out_grad.reshape(px, cols),
    )
    return output, weight_grad.reshape(3, 3, block, cols)


def fits(image_in, first_weight, second_weight):
    rows, width, depth = image_in.shape
    nz = lax.axis_size("cin")
    return (
        lax.axis_size("slab") == 4
        and lax.axis_size("cout") == 2
        and nz >= 2
        and nz % 2 == 0
        and rows % 2 == 0
        and width % 64 == 0
        and (rows * width) % (8 * nz) == 0
        and depth % 128 == 0
        and first_weight.shape[3] % 512 == 0
        and second_weight.shape[3] % 128 == 0
        and depth <= 512
        and second_weight.shape[3] <= 512
        and first_weight.shape[3] <= 1024
        and rows * width <= 512
    )


def padded_cells(cells):
    return jnp.pad(cells, ((1, 1), (1, 1), (0, 0)))


def conv(padded, weight):
    return lax.conv_general_dilated(
        padded[None],
        weight,
        (1, 1),
        "VALID",
        dimension_numbers=("NHWC", "HWIO", "NHWC"),
        precision=lax.Precision.HIGH,
        preferred_element_type=jnp.float32,
    )[0]


def on_device(image_in, first_weight, second_weight, out_grad):
    if fits(image_in, first_weight, second_weight):
        return fused(image_in, first_weight, second_weight, out_grad)
    slab = lax.axis_index("slab")
    block = first_weight.shape[3] // lax.axis_size("slab")
    first = lax.dynamic_slice_in_dim(first_weight, slab * block, block, axis=3)
    second = lax.dynamic_slice_in_dim(second_weight, slab * block, block, axis=2)
    image = lax.all_gather(image_in, "slab", axis=0, tiled=True)
    grad = lax.all_gather(out_grad, "slab", axis=0, tiled=True)
    rows, cols = image.shape[0], image.shape[1]
    hidden = jax.nn.silu(lax.psum(conv(padded_cells(image), first), "cin"))
    hidden_pad = padded_cells(hidden)
    part = conv(hidden_pad, second)
    part = lax.psum_scatter(part, "slab", scatter_dimension=0, tiled=True)
    output = lax.psum_scatter(part, "cout", scatter_dimension=1, tiled=True)
    flat_grad = grad.reshape(rows * cols, -1)
    grads = []
    for row_off in range(3):
        for col_off in range(3):
            window = hidden_pad[
                row_off : row_off + rows, col_off : col_off + cols, :
            ].reshape(rows * cols, -1)
            grads.append(
                lax.dot_general(
                    window,
                    flat_grad,
                    (((0,), (0,)), ((), ())),
                    precision=lax.Precision.HIGH,
                    preferred_element_type=jnp.float32,
                )
            )
    weight_grad = jnp.stack(grads).reshape(3, 3, block, flat_grad.shape[1])
    return (output, weight_grad)


def solution(mesh):
    in_specs = (
        P("slab", None, "cin"),
        P(None, None, "cin", "cout"),
        P(None, None, "cout", "cin"),
        P("slab", None, "cin"),
    )
    out_specs = (P("slab", "cout", "cin"), P(None, None, ("cout", "slab"), "cin"))
    return jax.shard_map(
        on_device, mesh=mesh, in_specs=in_specs, out_specs=out_specs, check_vma=False
    )
```
